32 devices in a mesh: dom: 4 (over y, core), aux: 8 (over z, x).
Axes of the slice: x: 2, y: 2, z: 4, core: 2. Of those that a mesh axis runs over, the one named last changes fastest.
Arguments:
- integrals: bfloat16 [4, 1024, 512, 128], P('dom', 'aux'), may hold values from -0.25 to 0.25
- density: bfloat16 [4, 4, 128, 128], P('dom'), may hold values from -0.25 to 0.25
- dens_cols: int32 [4, 4], replicated, may hold values from 0 to 3, as said below
- neighbours: int32 [4, 4], replicated, may hold values from 0 to 3, as said below
- metric: bfloat16 [4, 1024, 1024], P('dom', 'aux'), may hold values from -0.5 to 2.5, as said below
Outputs:
- exchange: float32 [4, 128, 128], P('dom')
The draws below stay inside these ranges and needn't reach their ends.
Inputs may be any that keep to these rules, and one draw needn't show every extreme that they name: `neighbours`: in each row the entries are distinct; position 0 holds the row's own block, the others are blocks within cyclic distance 2 of it, both blocks at distance 1 among them. `dens_cols`: in each row the entries are distinct; position 0 holds the row's own block, the others are blocks within cyclic distance 2 of it, both blocks at distance 1 among them. `metric`: each domain's matrix is symmetric.
All inputs are finite; a program needn't handle non-finite values.
Results may differ from the reference program's by a relative error of at most 0.004.
Values may be sent and summed in bfloat16 or wider, within the bound.
A program may use at most 128 MiB of HBM per device.

```python
import jax
import jax.numpy as jnp
from jax import lax

BS = 128
NAUX = 1024
NEI = 4
DT = 4
N_DOM = 4


def near_blocks(key, count):
    candidates = jnp.arange(1, N_DOM, dtype=jnp.int32)
    distance = jnp.minimum(candidates, N_DOM - candidates)
    jitter = jax.random.randint(key, (N_DOM, N_DOM - 1), 0, 1024, dtype=jnp.int32)
    scores = (distance[None, :] * 2048 + jitter) * N_DOM + candidates[None, :]
    unused, chosen_index = lax.top_k(-scores, count - 1)
    chosen = jnp.take(candidates, chosen_index)
    offsets = jnp.concatenate([jnp.zeros((N_DOM, 1), jnp.int32), chosen], axis=1)
    return ((jnp.arange(N_DOM, dtype=jnp.int32)[:, None] + offsets) % N_DOM).astype(jnp.int32)


def draw_neighbours(key, part):
    return near_blocks(jax.random.fold_in(key, 11), NEI)


def draw_dens_cols(key, part):
    return near_blocks(jax.random.fold_in(key, 23), DT)


def draw_metric(key, part):
    key_diag = jax.random.fold_in(key, 37)
    key_off = jax.random.fold_in(key, 41)
    diagonal = jnp.exp(jax.random.uniform(key_diag, (N_DOM, NAUX), jnp.float32, jnp.log(0.5), jnp.log(2.0)))
    off_diag = jax.random.truncated_normal(key_off, -4.0, 4.0, (N_DOM, NAUX, NAUX), jnp.float32)
    off_diag = off_diag * (0.5 / jnp.sqrt(jnp.float32(NAUX)))
    symmetric = (off_diag + jnp.swapaxes(off_diag, 1, 2)) * 0.7071
    return (symmetric + diagonal[:, :, None] * jnp.eye(NAUX, dtype=jnp.float32)[None]).astype(jnp.bfloat16)


def block_scale(own_key, extent, split, least, top_value):
    level, own = 1.0, jax.random.fold_in(own_key, 6)
    for dim, parts in split:
        draws = jnp.exp(jax.random.uniform(jax.random.fold_in(own, dim), (parts,), jnp.float32, least / len(split), top_value / len(split)))
        level = level * jnp.repeat(draws, extent[dim] // parts).reshape([-1 if axis == dim else 1 for axis in range(len(extent))])
    return level


def scatter_about(key, dims, scale, bound, split=(), kind=jnp.bfloat16):
    drawn = jax.random.normal(key, dims, jnp.float32) * scale
    if len(split) > 0:
        drawn = block_scale(key, dims, split, -0.22, 0.18) * drawn
    return jnp.clip(drawn, min=-bound, max=bound).astype(kind)


def setup_inputs(seed: int = 0) -> dict:
    arg_keys = jax.random.split(jax.random.key(seed), 6)
    integrals = scatter_about(arg_keys[0], (N_DOM, NAUX, NEI * BS, BS), (NEI * BS) ** -0.5, 0.25, ((0, 4), (1, 8)))
    density = scatter_about(arg_keys[1], (N_DOM, DT, BS, BS), (NEI * BS) ** -0.5, 0.25, ((0, 4),))
    dens_cols = draw_dens_cols(jax.random.fold_in(arg_keys[5], 71), 0)
    neighbours = draw_neighbours(jax.random.fold_in(arg_keys[5], 71), 0)
    metric = draw_metric(jax.random.fold_in(arg_keys[5], 71), 0)
    return {"integrals": integrals, "density": density, "dens_cols": dens_cols, "neighbours": neighbours, "metric": metric}


def local_density(listed_blocks, density, dens_cols):
    picked = jnp.take(density, listed_blocks, axis=0).astype(jnp.float32)
    tile_cols = jnp.take(dens_cols, listed_blocks, axis=0)
    matches = (tile_cols[:, None, :] == listed_blocks[None, :, None]).astype(jnp.float32)
    dense_tiles = jnp.einsum("jsk,jkab->jasb", matches, picked)
    return dense_tiles.reshape(NEI * BS, NEI * BS)


def reference(integrals, density, dens_cols, neighbours, metric):
    def one_domain(domain_items):
        integral_tile, metric_rows, listed_blocks = domain_items
        density_local = local_density(listed_blocks, density, dens_cols)
        wide_ints = integral_tile.astype(jnp.float32)
        half_product = jnp.einsum("ls,plm->psm", density_local, wide_ints).astype(jnp.bfloat16)
        fitted = jnp.einsum("qp,psm->qsm", metric_rows.astype(jnp.float32), wide_ints).astype(jnp.bfloat16)
        return jnp.einsum("psm,psn->mn", half_product.astype(jnp.float32), fitted.astype(jnp.float32))

    return lax.map(one_domain, (integrals, metric, neighbours))
```

```python
import functools

import jax
import jax.numpy as jnp
from jax import lax
from jax.experimental import pallas as pl
from jax.experimental.pallas import tpu as pltpu
from jax.sharding import PartitionSpec as P

RAD = 2
CHUNKS = 8
MESH = pl.DeviceIdType.MESH


def passed_along(block, axis, distance):
    devices = range(lax.axis_size(axis))
    route = [((i - distance) % len(devices), i) for i in devices]
    return lax.ppermute(block, axis, route)


def from_pair(block):
    return lax.ppermute(block, "dom", [(i ^ 1, i) for i in range(lax.axis_size("dom"))])


def move_kernel(n, i_ref, dt_ref, iout, hout, ibuf, held, stage,
                swap_send, swap_recv, i_send, i_recv, h_send, h_recv, loc, load):
    dom, aux = lax.axis_index("dom"), lax.axis_index("aux")
    half = n // 2
    core, side = dom % 2, aux // half
    base = dom - core
    partner = (base + 1 - core, (aux + half) % n)
    me = core * half + aux % half
    swaps = core != side
    block = jnp.where(swaps, (aux + half) % n, aux)
    rows, width = i_ref.shape[0], i_ref.shape[1]
    part, chunk = width // n, rows // CHUNKS

    def member(t):
        return (base + t // half, side * half + t % half)

    barrier = pltpu.get_barrier_semaphore()

    def greet(r, carry):
        pl.semaphore_signal(barrier, inc=1, device_id=member((me + r) % n), device_id_type=MESH)
        return carry

    lax.fori_loop(1, n, greet, 0)

    @pl.when(swaps)
    def _():
        pl.semaphore_signal(barrier, inc=1, device_id=partner, device_id_type=MESH)
        pl.semaphore_wait(barrier, n)

    @pl.when(jnp.logical_not(swaps))
    def _():
        pl.semaphore_wait(barrier, n - 1)

    def swap_copy(k):
        at = pl.ds(k * chunk, chunk)
        return pltpu.make_async_remote_copy(
            src_ref=i_ref.at[at], dst_ref=ibuf.at[at], send_sem=swap_send,
            recv_sem=swap_recv.at[k], device_id=partner, device_id_type=MESH)

    def spread(src, dst, at, send, recv):
        def one(r, carry):
            t = (me + r) % n
            pltpu.make_async_remote_copy(
                src_ref=src.at[at, pl.ds(pl.multiple_of(t * part, part), part)],
                dst_ref=dst.at[block, at],
                send_sem=send, recv_sem=recv,
                device_id=member(t), device_id_type=MESH).start()
            return carry
        lax.fori_loop(1, n, one, 0)

    def own(src, dst, at, sem):
        return pltpu.make_async_copy(
            src.at[at, pl.ds(pl.multiple_of(me * part, part), part)], dst.at[block, at], sem)

    def work(src, k):
        at = pl.ds(k * chunk, chunk)
        spread(src, iout, at, i_send, i_recv)
        own(src, iout, at, loc.at[0]).start()
        fetch = pltpu.make_async_copy(src.at[at], held, load)
        fetch.start()
        fetch.wait()

        def one(p, carry):
            stage[k * chunk + p] = jnp.dot(
                dt_ref[...], held[p], preferred_element_type=jnp.float32).astype(jnp.bfloat16)
            return carry
        lax.fori_loop(0, chunk, one, 0)
        spread(stage, hout, at, h_send, h_recv)
        own(stage, hout, at, loc.at[1]).start()

    @pl.when(swaps)
    def _():
        def begin(k, carry):
            swap_copy(k).start()
            return carry
        lax.fori_loop(0, CHUNKS, begin, 0)

        def step(k, carry):
            swap_copy(k).wait_recv()
            work(ibuf, k)
            return carry
        lax.fori_loop(0, CHUNKS, step, 0)
        pltpu.make_async_copy(i_ref, i_ref, swap_send).wait()

    @pl.when(jnp.logical_not(swaps))
    def _():
        def step(k, carry):
            work(i_ref, k)
            return carry
        lax.fori_loop(0, CHUNKS, step, 0)

    rest = pl.ds(0, n - 1)
    for out, s, r, l in ((iout, i_send, i_recv, 0), (hout, h_send, h_recv, 1)):
        pltpu.make_async_copy(out.at[0], out.at[0], loc.at[l]).wait()
        pltpu.make_async_copy(out.at[rest], out.at[rest], s).wait()
        pltpu.make_async_copy(out.at[rest], out.at[rest], r).wait()


def moved(ints, dt):
    n = lax.axis_size("aux")
    rows, width, cols = ints.shape
    shape = jax.ShapeDtypeStruct((n, rows, width // n, cols), ints.dtype)
    sem = pltpu.SemaphoreType.DMA
    return pl.pallas_call(
        functools.partial(move_kernel, n),
        out_shape=(shape, shape, jax.ShapeDtypeStruct(ints.shape, ints.dtype)),
        in_specs=[pl.BlockSpec(memory_space=pl.ANY), pl.BlockSpec(memory_space=pltpu.VMEM)],
        out_specs=[pl.BlockSpec(memory_space=pl.ANY)] * 3,
        scratch_shapes=[
            pltpu.VMEM((rows // CHUNKS, width, cols), ints.dtype),
            pltpu.VMEM((rows, width, cols), ints.dtype),
            sem, sem((CHUNKS,)), sem, sem, sem, sem, sem((2,)), sem,
        ],
        compiler_params=pltpu.CompilerParams(
            collective_id=0, has_side_effects=True, vmem_limit_bytes=40 * 2**20),
        cost_estimate=pl.CostEstimate(
            flops=2 * rows * width * width * cols, bytes_accessed=6 * rows * width * cols * 2,
            transcendentals=0),
    )(ints, dt)[:2]


def density_of(density, dens_cols, neighbours):
    domain_count = lax.axis_size("dom")
    my_domain = lax.axis_index("dom")
    size, count = density.shape[2], neighbours.shape[1]
    my_blocks = lax.dynamic_index_in_dim(neighbours, my_domain, 0, keepdims=False)
    slabs = jnp.stack([
        density[0] if offset == 0 else passed_along(density, "dom", -offset)[0]
        for offset in range(-RAD, RAD + 1)])
    slot = (my_blocks - my_domain + RAD) % domain_count
    listed = my_blocks[:, None] == jnp.arange(domain_count)[None]
    cols = jnp.sum(jnp.where(listed[:, :, None], dens_cols[None], 0), axis=1)
    matches = cols[:, None, :] == my_blocks[None, :, None]
    chosen = slot[:, None] == jnp.arange(2 * RAD + 1)[None]
    weight = (chosen[:, None, :, None] & matches[:, :, None, :]).astype(jnp.bfloat16)
    turned = jnp.einsum("jsok,okab->sbja", weight, slabs, preferred_element_type=jnp.float32)
    return turned.astype(jnp.bfloat16).reshape(count * size, count * size)


def body(integrals, density, dens_cols, neighbours, metric):
    n = lax.axis_size("aux")
    core, side = lax.axis_index("dom") % 2, lax.axis_index("aux") // (n // 2)
    stays = core == side
    mine = density_of(density, dens_cols, neighbours)
    dt = jnp.where(stays, mine, from_pair(mine))
    rows = lax.all_gather(metric[0], "aux", axis=0, tiled=True)
    rows = jnp.where(stays, rows, from_pair(rows))
    ints, half = moved(integrals[0], dt)
    ints = ints.reshape(-1, *ints.shape[2:])
    half = half.reshape(ints.shape)
    fitted = jnp.dot(
        rows, ints.reshape(ints.shape[0], -1), preferred_element_type=jnp.float32
    ).astype(jnp.bfloat16).reshape(ints.shape)
    part = jnp.einsum("psm,psn->mn", half, fitted, preferred_element_type=jnp.float32)
    spot = jnp.stack([jnp.where(side == 0, part, 0.0), jnp.where(side == 1, part, 0.0)])
    spot = lax.psum(spot, "aux")
    keep = jnp.where(core == 0, spot[0], spot[1])
    give = jnp.where(core == 0, spot[1], spot[0])
    return (keep + from_pair(give))[None]


def solution(mesh):
    return jax.shard_map(
        body,
        mesh=mesh,
        in_specs=(
            P("dom", "aux", None, None),
            P("dom", None, None, None),
            P(),
            P(),
            P("dom", "aux", None),
        ),
        out_specs=P("dom", None, None),
        check_vma=False,
    )
```

```python
import functools

import jax
import jax.numpy as jnp
from jax import lax
from jax.experimental import pallas as pl
from jax.experimental.pallas import tpu as pltpu
from jax.sharding import PartitionSpec as P

RAD = 2
CHUNKS = 8
MESH = pl.DeviceIdType.MESH


def passed_along(block, axis, distance):
    devices = range(lax.axis_size(axis))
    route = [((i - distance) % len(devices), i) for i in devices]
    return lax.ppermute(block, axis, route)


def from_pair(block):
    return lax.ppermute(block, "dom", [(i ^ 1, i) for i in range(lax.axis_size("dom"))])


def place(n):
    dom, aux = lax.axis_index("dom"), lax.axis_index("aux")
    half = n // 2
    core, side = dom % 2, aux // half
    base = dom - core
    partner = (base + 1 - core, (aux + half) % n)
    me = core * half + aux % half
    swaps = core != side
    block = jnp.where(swaps, (aux + half) % n, aux)

    def member(t):
        return (base + t // half, side * half + t % half)

    return partner, me, swaps, block, member


def meet(n, partner, me, swaps, member):
    barrier = pltpu.get_barrier_semaphore()

    def greet(r, carry):
        pl.semaphore_signal(barrier, inc=1, device_id=member((me + r) % n), device_id_type=MESH)
        return carry

    lax.fori_loop(1, n, greet, 0)

    @pl.when(swaps)
    def _():
        pl.semaphore_signal(barrier, inc=1, device_id=partner, device_id_type=MESH)
        pl.semaphore_wait(barrier, n)

    @pl.when(jnp.logical_not(swaps))
    def _():
        pl.semaphore_wait(barrier, n - 1)


def move_kernel(n, i_ref, dt_ref, m_ref, iout, hout, mout, ibuf, mbuf, held, stage,
                swap_send, swap_recv, i_send, i_recv, h_send, h_recv, loc, load,
                m_swap, m_send, m_recv, m_pair, m_loc):
    half = n // 2
    partner, me, swaps, block, member = place(n)
    rows, width = i_ref.shape[0], i_ref.shape[1]
    part, chunk = width // n, rows // CHUNKS
    meet(n, partner, me, swaps, member)
    other = member((me + half) % n)
    first = block // half * half

    def swap_metric():
        return pltpu.make_async_remote_copy(
            src_ref=m_ref, dst_ref=mbuf, send_sem=m_swap.at[0], recv_sem=m_swap.at[1],
            device_id=partner, device_id_type=MESH)

    def spread_metric(src):
        pltpu.make_async_copy(src, mout.at[block], m_loc).start()

        def one(r, carry):
            t = me // half * half + (me + r) % half
            pltpu.make_async_remote_copy(
                src_ref=src, dst_ref=mout.at[block], send_sem=m_send, recv_sem=m_recv,
                device_id=member(t), device_id_type=MESH).start()
            return carry
        lax.fori_loop(1, half, one, 0)

    def swap_copy(k):
        at = pl.ds(k * chunk, chunk)
        return pltpu.make_async_remote_copy(
            src_ref=i_ref.at[at], dst_ref=ibuf.at[at], send_sem=swap_send,
            recv_sem=swap_recv.at[k], device_id=partner, device_id_type=MESH)

    def spread(src, dst, at, send, recv):
        def one(r, carry):
            t = (me + r) % n
            pltpu.make_async_remote_copy(
                src_ref=src.at[at, pl.ds(pl.multiple_of(t * part, part), part)],
                dst_ref=dst.at[block, at],
                send_sem=send, recv_sem=recv,
                device_id=member(t), device_id_type=MESH).start()
            return carry
        lax.fori_loop(1, n, one, 0)

    def own(src, dst, at, sem):
        return pltpu.make_async_copy(
            src.at[at, pl.ds(pl.multiple_of(me * part, part), part)], dst.at[block, at], sem)

    def work(src, k):
        at = pl.ds(k * chunk, chunk)
        spread(src, iout, at, i_send, i_recv)
        own(src, iout, at, loc.at[0]).start()
        fetch = pltpu.make_async_copy(src.at[at], held, load)
        fetch.start()
        fetch.wait()

        def one(p, carry):
            stage[k * chunk + p] = jnp.dot(
                dt_ref[...], held[p], preferred_element_type=jnp.float32).astype(jnp.bfloat16)
            return carry
        lax.fori_loop(0, chunk, one, 0)
        spread(stage, hout, at, h_send, h_recv)
        own(stage, hout, at, loc.at[1]).start()

    @pl.when(swaps)
    def _():
        swap_metric().start()

        def begin(k, carry):
            swap_copy(k).start()
            return carry
        lax.fori_loop(0, CHUNKS, begin, 0)
        swap_metric().wait()
        spread_metric(mbuf)

        def step(k, carry):
            swap_copy(k).wait_recv()
            work(ibuf, k)
            return carry
        lax.fori_loop(0, CHUNKS, step, 0)
        pltpu.make_async_copy(i_ref, i_ref, swap_send).wait()

    @pl.when(jnp.logical_not(swaps))
    def _():
        spread_metric(m_ref)

        def step(k, carry):
            work(i_ref, k)
            return carry
        lax.fori_loop(0, CHUNKS, step, 0)

    pltpu.make_async_copy(m_ref, mout.at[block], m_loc).wait()
    few = mout.at[pl.ds(0, half - 1)]
    pltpu.make_async_copy(few, few, m_send).wait()
    pltpu.make_async_copy(few, few, m_recv).wait()
    lot = mout.at[pl.ds(first, half)]
    share = pltpu.make_async_remote_copy(
        src_ref=lot, dst_ref=lot, send_sem=m_pair.at[0], recv_sem=m_pair.at[1],
        device_id=other, device_id_type=MESH)
    share.start()
    share.wait()

    rest = pl.ds(0, n - 1)
    for out, s, r, l in ((iout, i_send, i_recv, 0), (hout, h_send, h_recv, 1)):
        pltpu.make_async_copy(out.at[0], out.at[0], loc.at[l]).wait()
        pltpu.make_async_copy(out.at[rest], out.at[rest], s).wait()
        pltpu.make_async_copy(out.at[rest], out.at[rest], r).wait()


def sum_kernel(n, e_ref, out_ref, parts, total, swap, send, recv):
    partner, me, swaps, block, member = place(n)
    meet(n, partner, me, swaps, member)

    def one(r, carry):
        pltpu.make_async_remote_copy(
            src_ref=e_ref, dst_ref=parts.at[me], send_sem=send, recv_sem=recv,
            device_id=member((me + r) % n), device_id_type=MESH).start()
        return carry
    lax.fori_loop(1, n, one, 0)
    parts[me] = e_ref[...]
    rest = parts.at[pl.ds(0, n - 1)]
    pltpu.make_async_copy(rest, rest, recv).wait()
    pltpu.make_async_copy(rest, rest, send).wait()
    total[...] = parts[0]

    def add(t, carry):
        total[...] += parts[t]
        return carry
    lax.fori_loop(1, n, add, 0)

    @pl.when(swaps)
    def _():
        copy = pltpu.make_async_remote_copy(
            src_ref=total, dst_ref=out_ref, send_sem=swap.at[0], recv_sem=swap.at[1],
            device_id=partner, device_id_type=MESH)
        copy.start()
        copy.wait()

    @pl.when(jnp.logical_not(swaps))
    def _():
        out_ref[...] = total[...]


def summed(part):
    n = lax.axis_size("aux")
    sem = pltpu.SemaphoreType.DMA
    vmem = pl.BlockSpec(memory_space=pltpu.VMEM)
    return pl.pallas_call(
        functools.partial(sum_kernel, n),
        out_shape=jax.ShapeDtypeStruct(part.shape, part.dtype),
        in_specs=[vmem],
        out_specs=vmem,
        scratch_shapes=[
            pltpu.VMEM((n, *part.shape), part.dtype), pltpu.VMEM(part.shape, part.dtype),
            sem((2,)), sem, sem],
        compiler_params=pltpu.CompilerParams(collective_id=1, has_side_effects=True),
    )(part)


def moved(ints, dt, metric):
    n = lax.axis_size("aux")
    rows, width, cols = ints.shape
    shape = jax.ShapeDtypeStruct((n, rows, width // n, cols), ints.dtype)
    sem = pltpu.SemaphoreType.DMA
    return pl.pallas_call(
        functools.partial(move_kernel, n),
        out_shape=(
            shape, shape, jax.ShapeDtypeStruct((n, *metric.shape), metric.dtype),
            jax.ShapeDtypeStruct(ints.shape, ints.dtype),
            jax.ShapeDtypeStruct(metric.shape, metric.dtype)),
        in_specs=[
            pl.BlockSpec(memory_space=pl.ANY), pl.BlockSpec(memory_space=pltpu.VMEM),
            pl.BlockSpec(memory_space=pl.ANY)],
        out_specs=[pl.BlockSpec(memory_space=pl.ANY)] * 5,
        scratch_shapes=[
            pltpu.VMEM((rows // CHUNKS, width, cols), ints.dtype),
            pltpu.VMEM((rows, width, cols), ints.dtype),
            sem, sem((CHUNKS,)), sem, sem, sem, sem, sem((2,)), sem,
            sem((2,)), sem, sem, sem((2,)), sem,
        ],
        compiler_params=pltpu.CompilerParams(
            collective_id=0, has_side_effects=True, vmem_limit_bytes=40 * 2**20),
        cost_estimate=pl.CostEstimate(
            flops=2 * rows * width * width * cols, bytes_accessed=6 * rows * width * cols * 2,
            transcendentals=0),
    )(ints, dt, metric)[:3]


def density_of(density, dens_cols, neighbours):
    domain_count = lax.axis_size("dom")
    my_domain = lax.axis_index("dom")
    size, count = density.shape[2], neighbours.shape[1]
    my_blocks = lax.dynamic_index_in_dim(neighbours, my_domain, 0, keepdims=False)
    slabs = jnp.stack([
        density[0] if offset == 0 else passed_along(density, "dom", -offset)[0]
        for offset in range(-RAD, RAD + 1)])
    slot = (my_blocks - my_domain + RAD) % domain_count
    listed = my_blocks[:, None] == jnp.arange(domain_count)[None]
    cols = jnp.sum(jnp.where(listed[:, :, None], dens_cols[None], 0), axis=1)
    matches = cols[:, None, :] == my_blocks[None, :, None]
    chosen = slot[:, None] == jnp.arange(2 * RAD + 1)[None]
    weight = (chosen[:, None, :, None] & matches[:, :, None, :]).astype(jnp.bfloat16)
    turned = jnp.einsum("jsok,okab->sbja", weight, slabs, preferred_element_type=jnp.float32)
    return turned.astype(jnp.bfloat16).reshape(count * size, count * size)


def body(integrals, density, dens_cols, neighbours, metric):
    n = lax.axis_size("aux")
    core, side = lax.axis_index("dom") % 2, lax.axis_index("aux") // (n // 2)
    stays = core == side
    mine = density_of(density, dens_cols, neighbours)
    dt = jnp.where(stays, mine, from_pair(mine))
    ints, half, rows = moved(integrals[0], dt, metric[0])
    rows = rows.reshape(-1, rows.shape[2])
    ints = ints.reshape(-1, *ints.shape[2:])
    half = half.reshape(ints.shape)
    fitted = jnp.dot(
        rows, ints.reshape(ints.shape[0], -1), preferred_element_type=jnp.float32
    ).astype(jnp.bfloat16).reshape(ints.shape)
    part = jnp.einsum("psm,psn->mn", half, fitted, preferred_element_type=jnp.float32)
    return summed(part)[None]


def solution(mesh):
    return jax.shard_map(
        body,
        mesh=mesh,
        in_specs=(
            P("dom", "aux", None, None),
            P("dom", None, None, None),
            P(),
            P(),
            P("dom", "aux", None),
        ),
        out_specs=P("dom", None, None),
        check_vma=False,
    )
```

```python
import functools

import jax
import jax.numpy as jnp
from jax import lax
from jax.experimental import pallas as pl
from jax.experimental.pallas import tpu as pltpu
from jax.sharding import PartitionSpec as P

RAD = 2
CHUNKS = 8
MESH = pl.DeviceIdType.MESH


def passed_along(block, axis, distance):
    devices = range(lax.axis_size(axis))
    route = [((i - distance) % len(devices), i) for i in devices]
    return lax.ppermute(block, axis, route)


def from_pair(block):
    return lax.ppermute(block, "dom", [(i ^ 1, i) for i in range(lax.axis_size("dom"))])


def place(n):
    dom, aux = lax.axis_index("dom"), lax.axis_index("aux")
    half = n // 2
    core, side = dom % 2, aux // half
    base = dom - core
    partner = (base + 1 - core, (aux + half) % n)
    me = core * half + aux % half
    swaps = core != side
    block = jnp.where(swaps, (aux + half) % n, aux)

    def member(t):
        return (base + t // half, side * half + t % half)

    return partner, me, swaps, block, member


def meet(n, partner, me, swaps, member):
    barrier = pltpu.get_barrier_semaphore()

    def greet(r, carry):
        pl.semaphore_signal(barrier, inc=1, device_id=member((me + r) % n), device_id_type=MESH)
        return carry

    lax.fori_loop(1, n, greet, 0)

    @pl.when(swaps)
    def _():
        pl.semaphore_signal(barrier, inc=1, device_id=partner, device_id_type=MESH)
        pl.semaphore_wait(barrier, n)

    @pl.when(jnp.logical_not(swaps))
    def _():
        pl.semaphore_wait(barrier, n - 1)


def move_kernel(n, i_ref, dt_ref, m_ref, iout, hout, mout, ibuf, mbuf, held, stage,
                swap_send, swap_recv, i_send, i_recv, h_send, h_recv, loc, load,
                m_swap, m_send, m_recv, m_pair, m_loc):
    half = n // 2
    partner, me, swaps, block, member = place(n)
    rows, width = i_ref.shape[0], i_ref.shape[1]
    part, chunk = width // n, rows // CHUNKS
    meet(n, partner, me, swaps, member)
    other = member((me + half) % n)
    first = block // half * half

    def swap_metric():
        return pltpu.make_async_remote_copy(
            src_ref=m_ref, dst_ref=mbuf, send_sem=m_swap.at[0], recv_sem=m_swap.at[1],
            device_id=partner, device_id_type=MESH)

    def spread_metric(src):
        pltpu.make_async_copy(src, mout.at[block], m_loc).start()

        def one(r, carry):
            t = me // half * half + (me + r) % half
            pltpu.make_async_remote_copy(
                src_ref=src, dst_ref=mout.at[block], send_sem=m_send, recv_sem=m_recv,
                device_id=member(t), device_id_type=MESH).start()
            return carry
        lax.fori_loop(1, half, one, 0)

    def swap_copy(k):
        at = pl.ds(k * chunk, chunk)
        return pltpu.make_async_remote_copy(
            src_ref=i_ref.at[at], dst_ref=ibuf.at[at], send_sem=swap_send,
            recv_sem=swap_recv.at[k], device_id=partner, device_id_type=MESH)

    def spread(src, dst, at, send, recv):
        def one(r, carry):
            t = (me + r) % n
            pltpu.make_async_remote_copy(
                src_ref=src.at[at, pl.ds(pl.multiple_of(t * part, part), part)],
                dst_ref=dst.at[block, at],
                send_sem=send, recv_sem=recv,
                device_id=member(t), device_id_type=MESH).start()
            return carry
        lax.fori_loop(1, n, one, 0)

    def own(src, dst, at, sem):
        return pltpu.make_async_copy(
            src.at[at, pl.ds(pl.multiple_of(me * part, part), part)], dst.at[block, at], sem)

    def work(src, k):
        at = pl.ds(k * chunk, chunk)
        spread(src, iout, at, i_send, i_recv)
        own(src, iout, at, loc.at[0]).start()
        fetch = pltpu.make_async_copy(src.at[at], held, load)
        fetch.start()
        fetch.wait()

        def one(p, carry):
            stage[k * chunk + p] = jnp.dot(
                dt_ref[...], held[p], preferred_element_type=jnp.float32).astype(jnp.bfloat16)
            return carry
        lax.fori_loop(0, chunk, one, 0)
        spread(stage, hout, at, h_send, h_recv)
        own(stage, hout, at, loc.at[1]).start()

    @pl.when(swaps)
    def _():
        swap_metric().start()

        def begin(k, carry):
            swap_copy(k).start()
            return carry
        lax.fori_loop(0, CHUNKS, begin, 0)
        swap_metric().wait()
        spread_metric(mbuf)

        def step(k, carry):
            swap_copy(k).wait_recv()
            work(ibuf, k)
            return carry
        lax.fori_loop(0, CHUNKS, step, 0)
        pltpu.make_async_copy(i_ref, i_ref, swap_send).wait()

    @pl.when(jnp.logical_not(swaps))
    def _():
        spread_metric(m_ref)

        def step(k, carry):
            work(i_ref, k)
            return carry
        lax.fori_loop(0, CHUNKS, step, 0)

    pltpu.make_async_copy(m_ref, mout.at[block], m_loc).wait()
    few = mout.at[pl.ds(0, half - 1)]
    pltpu.make_async_copy(few, few, m_send).wait()
    pltpu.make_async_copy(few, few, m_recv).wait()
    lot = mout.at[pl.ds(first, half)]
    share = pltpu.make_async_remote_copy(
        src_ref=lot, dst_ref=lot, send_sem=m_pair.at[0], recv_sem=m_pair.at[1],
        device_id=other, device_id_type=MESH)
    share.start()
    share.wait()

    rest = pl.ds(0, n - 1)
    for out, s, r, l in ((iout, i_send, i_recv, 0), (hout, h_send, h_recv, 1)):
        pltpu.make_async_copy(out.at[0], out.at[0], loc.at[l]).wait()
        pltpu.make_async_copy(out.at[rest], out.at[rest], s).wait()
        pltpu.make_async_copy(out.at[rest], out.at[rest], r).wait()


def sum_kernel(n, e_ref, out_ref, parts, total, swap, send, recv):
    partner, me, swaps, block, member = place(n)
    meet(n, partner, me, swaps, member)

    def one(r, carry):
        pltpu.make_async_remote_copy(
            src_ref=e_ref, dst_ref=parts.at[me], send_sem=send, recv_sem=recv,
            device_id=member((me + r) % n), device_id_type=MESH).start()
        return carry
    lax.fori_loop(1, n, one, 0)
    parts[me] = e_ref[...]
    rest = parts.at[pl.ds(0, n - 1)]
    pltpu.make_async_copy(rest, rest, recv).wait()
    pltpu.make_async_copy(rest, rest, send).wait()
    total[...] = parts[0]

    def add(t, carry):
        total[...] += parts[t]
        return carry
    lax.fori_loop(1, n, add, 0)

    @pl.when(swaps)
    def _():
        copy = pltpu.make_async_remote_copy(
            src_ref=total, dst_ref=out_ref, send_sem=swap.at[0], recv_sem=swap.at[1],
            device_id=partner, device_id_type=MESH)
        copy.start()
        copy.wait()

    @pl.when(jnp.logical_not(swaps))
    def _():
        out_ref[...] = total[...]


def summed(part):
    n = lax.axis_size("aux")
    sem = pltpu.SemaphoreType.DMA
    vmem = pl.BlockSpec(memory_space=pltpu.VMEM)
    return pl.pallas_call(
        functools.partial(sum_kernel, n),
        out_shape=jax.ShapeDtypeStruct(part.shape, part.dtype),
        in_specs=[vmem],
        out_specs=vmem,
        scratch_shapes=[
            pltpu.VMEM((n, *part.shape), part.dtype), pltpu.VMEM(part.shape, part.dtype),
            sem((2,)), sem, sem],
        compiler_params=pltpu.CompilerParams(collective_id=1, has_side_effects=True),
    )(part)


def moved(ints, dt, metric):
    n = lax.axis_size("aux")
    rows, width, cols = ints.shape
    shape = jax.ShapeDtypeStruct((n, rows, width // n, cols), ints.dtype)
    sem = pltpu.SemaphoreType.DMA
    return pl.pallas_call(
        functools.partial(move_kernel, n),
        out_shape=(
            shape, shape, jax.ShapeDtypeStruct((n, *metric.shape), metric.dtype),
            jax.ShapeDtypeStruct(ints.shape, ints.dtype),
            jax.ShapeDtypeStruct(metric.shape, metric.dtype)),
        in_specs=[
            pl.BlockSpec(memory_space=pl.ANY), pl.BlockSpec(memory_space=pltpu.VMEM),
            pl.BlockSpec(memory_space=pl.ANY)],
        out_specs=[pl.BlockSpec(memory_space=pl.ANY)] * 5,
        scratch_shapes=[
            pltpu.VMEM((rows // CHUNKS, width, cols), ints.dtype),
            pltpu.VMEM((rows, width, cols), ints.dtype),
            sem, sem((CHUNKS,)), sem, sem, sem, sem, sem((2,)), sem,
            sem((2,)), sem, sem, sem((2,)), sem,
        ],
        compiler_params=pltpu.CompilerParams(
            collective_id=0, has_side_effects=True, vmem_limit_bytes=40 * 2**20),
        cost_estimate=pl.CostEstimate(
            flops=2 * rows * width * width * cols, bytes_accessed=6 * rows * width * cols * 2,
            transcendentals=0),
    )(ints, dt, metric)[:3]


def share_kernel(m_ref, i_ref, h_ref, e_ref):
    @pl.when(pl.program_id(0) == 0)
    def _():
        e_ref[...] = jnp.zeros_like(e_ref)

    ints = jnp.swapaxes(i_ref[...], 0, 1)
    half = jnp.swapaxes(h_ref[...], 0, 1)
    cols = ints.shape[2]
    total = jnp.zeros(e_ref.shape, jnp.float32)
    for s in range(0, ints.shape[0], 2):
        pair = jnp.concatenate([ints[s], ints[s + 1]], axis=1)
        fitted = jnp.dot(
            m_ref[...], pair, preferred_element_type=jnp.float32).astype(jnp.bfloat16)
        for o in range(2):
            total += lax.dot_general(
                half[s + o], fitted[:, o * cols:(o + 1) * cols], (((0,), (0,)), ((), ())),
                preferred_element_type=jnp.float32)
    e_ref[...] += total


def share_of(rows, ints, half):
    count, width, cols = ints.shape
    step = min(16, width)
    block = pl.BlockSpec((count, step, cols), lambda s: (0, s, 0))
    return pl.pallas_call(
        share_kernel,
        grid=(width // step,),
        out_shape=jax.ShapeDtypeStruct((cols, cols), jnp.float32),
        in_specs=[pl.BlockSpec(memory_space=pltpu.VMEM), block, block],
        out_specs=pl.BlockSpec((cols, cols), lambda s: (0, 0)),
        compiler_params=pltpu.CompilerParams(vmem_limit_bytes=56 * 2**20),
    )(rows, ints, half)


def density_of(density, dens_cols, neighbours):
    domain_count = lax.axis_size("dom")
    my_domain = lax.axis_index("dom")
    size, count = density.shape[2], neighbours.shape[1]
    my_blocks = lax.dynamic_index_in_dim(neighbours, my_domain, 0, keepdims=False)
    slabs = jnp.stack([
        density[0] if offset == 0 else passed_along(density, "dom", -offset)[0]
        for offset in range(-RAD, RAD + 1)])
    slot = (my_blocks - my_domain + RAD) % domain_count
    listed = my_blocks[:, None] == jnp.arange(domain_count)[None]
    cols = jnp.sum(jnp.where(listed[:, :, None], dens_cols[None], 0), axis=1)
    matches = cols[:, None, :] == my_blocks[None, :, None]
    chosen = slot[:, None] == jnp.arange(2 * RAD + 1)[None]
    weight = (chosen[:, None, :, None] & matches[:, :, None, :]).astype(jnp.bfloat16)
    turned = jnp.einsum("jsok,okab->sbja", weight, slabs, preferred_element_type=jnp.float32)
    return turned.astype(jnp.bfloat16).reshape(count * size, count * size)


def body(integrals, density, dens_cols, neighbours, metric):
    n = lax.axis_size("aux")
    core, side = lax.axis_index("dom") % 2, lax.axis_index("aux") // (n // 2)
    stays = core == side
    mine = density_of(density, dens_cols, neighbours)
    dt = jnp.where(stays, mine, from_pair(mine))
    ints, half, rows = moved(integrals[0], dt, metric[0])
    rows = rows.reshape(-1, rows.shape[2])
    part = share_of(rows, ints.reshape(-1, *ints.shape[2:]), half.reshape(-1, *half.shape[2:]))
    return summed(part)[None]


def solution(mesh):
    return jax.shard_map(
        body,
        mesh=mesh,
        in_specs=(
            P("dom", "aux", None, None),
            P("dom", None, None, None),
            P(),
            P(),
            P("dom", "aux", None),
        ),
        out_specs=P("dom", None, None),
        check_vma=False,
    )
```
